32 devices in a mesh: head: 2 (over y), frame: 16 (over z, x, core).
Axes of the slice: x: 2, y: 2, z: 4, core: 2. Of those that a mesh axis runs over, the one named last changes fastest.
Arguments:
- queries: bfloat16 [16384, 16, 128], P(('frame', 'head')), may hold values from -30 to 30
- keys: bfloat16 [16384, 16, 128], P(('frame', 'head')), may hold values from -4 to 4
- values: bfloat16 [16384, 16, 128], P(('frame', 'head')), may hold values from -24 to 24
- block_mask: int32 [16, 16, 16], replicated, may hold values from 0 to 1, as said below
- strides: int32 [16], replicated, may hold values from 1 to 16, as said below
- offsets: int32 [16], replicated, may hold values from 0 to 15
Outputs:
- attended: bfloat16 [16384, 16, 128], P(('frame', 'head'))
The draws below stay inside these ranges and needn't reach their ends.
Inputs may be any that keep to these rules, and one draw needn't show every extreme that they name: Every diagonal entry block_mask[i, b, b] is 1. strides[0] is 1, strides[1] is 4, 8 or 16, and every later entry is 8 or 16.
All inputs are finite; a program needn't handle non-finite values.
Results may differ from the reference program's by a relative error of at most 0.0043.
Values may be sent and summed in bfloat16 or wider, within the bound.
A program may use at most 128 MiB of HBM per device.

```python
import jax
import jax.numpy as jnp
from jax import lax

HD = 128
HEADS = 16
BLOCK = 64
TPF = 1024
FRAMES = 16
TOKENS = 16384


def integer_tables(key):
    frame_blocks = TPF // BLOCK
    offsets = jax.random.randint(jax.random.fold_in(key, 11), (FRAMES,), 0, frame_blocks)
    levels = jax.random.randint(jax.random.fold_in(key, 12), (FRAMES, 1, 1), 1, 8)
    coins = jax.random.randint(jax.random.fold_in(key, 13), (FRAMES, frame_blocks, frame_blocks), 0, 8)
    full_rows = jax.random.randint(jax.random.fold_in(key, 14), (FRAMES,), 0, frame_blocks)
    row_ids = jnp.arange(frame_blocks)[None, :, None]
    col_ids = jnp.arange(frame_blocks)[None, None, :]
    block_mask = ((coins < levels) | (row_ids == col_ids) | (row_ids == full_rows[:, None, None])).astype(jnp.int32)
    first_pick = jax.random.randint(jax.random.fold_in(key, 15), (), 0, 3)
    later_picks = jax.random.randint(jax.random.fold_in(key, 16), (FRAMES,), 0, 2)
    first_value = jnp.where(first_pick == 0, frame_blocks // 4, jnp.where(first_pick == 1, frame_blocks // 2, frame_blocks))
    later_values = jnp.where(later_picks == 0, frame_blocks // 2, frame_blocks)
    distances = jnp.arange(FRAMES)
    strides = jnp.where(distances == 0, 1, jnp.where(distances == 1, first_value, later_values)).astype(jnp.int32)
    return (offsets.astype(jnp.int32), block_mask, strides)


def attention_inputs(key):
    frame_blocks = TPF // BLOCK
    layout = (FRAMES, frame_blocks, BLOCK, HEADS, HD)
    query_draw = jnp.clip(jax.random.normal(jax.random.fold_in(key, 21), layout, jnp.float32), -4.0, 4.0)
    key_draw = jnp.clip(jax.random.normal(jax.random.fold_in(key, 22), layout, jnp.float32), -4.0, 4.0)
    shape = (FRAMES * TPF, HEADS, HD)
    return (query_draw.reshape(shape), key_draw.reshape(shape))


def draw_queries(key, part):
    return attention_inputs(key)[0].astype(jnp.bfloat16)


def draw_keys(key, part):
    return attention_inputs(key)[1].astype(jnp.bfloat16)


def draw_block_mask(key, part):
    return integer_tables(key)[1]


def draw_strides(key, part):
    return integer_tables(key)[2]


def draw_offsets(key, part):
    return integer_tables(key)[0]


def level_of(rng, dims, pieces, smallest, top_value):
    def one(position, blocks):
        heights = jax.random.uniform(jax.random.fold_in(jax.random.fold_in(rng, 6), position), (blocks,), jnp.float32, smallest / len(pieces), top_value / len(pieces))
        return jnp.repeat(jnp.exp(heights), dims[position] // blocks).reshape((-1,) + (1,) * (len(dims) - position - 1))

    loudness = one(*pieces[0])
    for cut in pieces[1:]:
        loudness = loudness * one(*cut)
    return loudness


def centred(rng, extent, scale, reach, pieces=(), kind=jnp.bfloat16):
    gain = level_of(rng, extent, pieces, -0.22, 0.18) if pieces else 1.0
    drawn = jax.random.normal(rng, extent, jnp.float32) * scale * gain
    return jnp.minimum(jnp.maximum(drawn, -reach), reach).astype(kind)


def setup_inputs(seed: int = 0) -> dict:
    streams_of = jax.random.split(jax.random.key(seed), 7)
    return {
        "queries": draw_queries(jax.random.fold_in(streams_of[6], 71), 0),
        "keys": draw_keys(jax.random.fold_in(streams_of[6], 71), 0),
        "values": centred(streams_of[2], (TOKENS, HEADS, HD), 4.0, 24.0, ((0, 32),)),
        "block_mask": draw_block_mask(jax.random.fold_in(streams_of[6], 71), 0),
        "strides": draw_strides(jax.random.fold_in(streams_of[6], 71), 0),
        "offsets": draw_offsets(jax.random.fold_in(streams_of[6], 71), 0),
    }


masked_score = -1.0e30


def group_terms(query_blocks, key_rows, value_rows, keep_mask, score_scale):
    query_wide = query_blocks.astype(jnp.float32)
    key_wide = key_rows.astype(jnp.float32)
    scores = jnp.einsum("qahd,gnhd->hqagn", query_wide, key_wide) * score_scale
    allowed = keep_mask[None, :, None, :, :]
    scores = jnp.where(allowed, scores, masked_score)
    group_tops = jnp.max(scores, axis=4)
    weights = jnp.where(allowed, jnp.exp(scores - group_tops[..., None]), 0.0)
    group_totals = jnp.sum(weights, axis=4)
    rounded = lax.optimization_barrier(weights.astype(jnp.bfloat16)).astype(jnp.float32)
    group_sums = jnp.einsum("hqagn,gnhd->hqagd", rounded, value_rows.astype(jnp.float32))
    return group_tops, group_totals, group_sums


def reference(queries, keys, values, block_mask, strides, offsets):
    frame_blocks = TPF // BLOCK
    score_scale = HD ** -0.5
    layout = (FRAMES, frame_blocks, BLOCK, HEADS, HD)
    query_all = queries.reshape(layout)
    key_all = keys.reshape(layout)
    value_all = values.reshape(layout)
    frame_ids = jnp.arange(FRAMES, dtype=jnp.int32)
    anchors = (frame_blocks - offsets % frame_blocks) % frame_blocks
    anchor_keys = key_all[frame_ids, anchors]
    anchor_values = value_all[frame_ids, anchors]

    def one_frame(frame_index):
        query_blocks = query_all[frame_index]
        own_mask = block_mask[frame_index] == 1
        results = []
        keep_mask = jnp.repeat(own_mask, BLOCK, axis=1)[:, None, :]
        results.append(group_terms(query_blocks, key_all[frame_index].reshape(1, TPF, HEADS, HD),
                                   value_all[frame_index].reshape(1, TPF, HEADS, HD), keep_mask, score_scale))
        for distance in (1, 2, 3):
            spacing = frame_blocks // 4 if distance == 1 else frame_blocks // 2
            block_count = frame_blocks // spacing
            for direction in (1, -1):
                source_frame = frame_index - direction * distance
                valid = (source_frame >= 0) & (source_frame < FRAMES)
                clipped = jnp.clip(source_frame, 0, FRAMES - 1)
                chosen = (spacing - offsets[clipped] % spacing) % spacing + spacing * jnp.arange(block_count, dtype=jnp.int32)
                phase_ok = ((chosen + offsets[clipped]) % strides[distance]) == 0
                kept = valid & own_mask[:, chosen] & phase_ok[None, :]
                keep_mask = jnp.repeat(kept, BLOCK, axis=1)[:, None, :]
                chosen_keys = key_all[clipped][chosen].reshape(1, block_count * BLOCK, HEADS, HD)
                chosen_values = value_all[clipped][chosen].reshape(1, block_count * BLOCK, HEADS, HD)
                results.append(group_terms(query_blocks, chosen_keys, chosen_values, keep_mask, score_scale))
        distances = jnp.abs(frame_index - frame_ids)
        phase_ok = ((anchors + offsets) % strides[distances]) == 0
        kept = (distances >= 4)[None, :] & own_mask[:, anchors] & phase_ok[None, :]
        keep_mask = jnp.repeat(kept, BLOCK, axis=1).reshape(frame_blocks, FRAMES, BLOCK)
        results.append(group_terms(query_blocks, anchor_keys, anchor_values, keep_mask, score_scale))
        group_tops = jnp.concatenate([entry[0] for entry in results], axis=3)
        group_totals = jnp.concatenate([entry[1] for entry in results], axis=3)
        group_sums = jnp.concatenate([entry[2] for entry in results], axis=3)
        overall_top = jnp.max(group_tops, axis=3)
        factors = jnp.exp(group_tops - overall_top[..., None])
        denominator = jnp.sum(factors * group_totals, axis=3)
        numerator = jnp.sum(factors[..., None] * group_sums, axis=3)
        output = (numerator / denominator[..., None]).astype(jnp.bfloat16)
        return jnp.transpose(output, (1, 2, 0, 3))

    result = lax.map(one_frame, frame_ids)
    return result.reshape(FRAMES * TPF, HEADS, HD)
```

```python
import functools
import math

import jax
import jax.numpy as jnp
from jax import lax
from jax.experimental import pallas as pl
from jax.experimental.pallas import tpu as pltpu
from jax.sharding import PartitionSpec as P

masked_score = -1e30
lanes = 128
vmem_bytes = 48 * 1024 * 1024


def rotated(block, axis, shift):
    size = lax.axis_size(axis)
    return lax.ppermute(block, axis, [(i, (i + shift) % size) for i in range(size)])


def passed_along(block, axis, distance):
    devices = range(lax.axis_size(axis))
    route = [(i - distance, i) for i in devices if i - distance in devices]
    return lax.ppermute(block, axis, route)


def query_rows(q_ref, start, first_row, tile, block_rows):
    query = q_ref[start : start + tile, :]
    row = lax.broadcasted_iota(jnp.int32, (tile, lanes), 0) + first_row
    lane = lax.broadcasted_iota(jnp.int32, (tile, lanes), 1)
    marks = jnp.where(row // block_rows == lane, 1.0, 0.0).astype(jnp.bfloat16)
    return jnp.concatenate([query, marks], axis=1)


def score_tile(query_marked, keys_marked):
    return lax.dot_general(
        query_marked, keys_marked, (((1,), (1,)), ((), ())), preferred_element_type=jnp.float32
    )


def own_kernel(parts, tile, block_rows, factor, start_ref, bias_ref, *refs):
    q_refs, k_refs, v_refs = refs[:parts], refs[parts : 2 * parts], refs[2 * parts : 3 * parts]
    state_ref = refs[3 * parts]
    key_rows = jnp.concatenate([ref[...] for ref in k_refs], axis=0)
    value_rows = jnp.concatenate([ref[...] for ref in v_refs], axis=0)
    keys_marked = jnp.concatenate([key_rows, bias_ref[...]], axis=1)
    values_ones = jnp.concatenate([value_rows, jnp.ones_like(value_rows)], axis=1)
    rows, head_dim = q_refs[0].shape
    for part in range(parts):
        for start in range(0, rows, tile):
            first_row = part * rows + start
            marked = query_rows(q_refs[part], start, first_row, tile, block_rows)
            scores = score_tile(marked, keys_marked)
            top = jnp.max(scores, axis=1, keepdims=True)
            weights = jnp.exp2(scores * factor - top * factor).astype(jnp.bfloat16)
            sums = jnp.dot(weights, values_ones, preferred_element_type=jnp.float32)
            lane = lax.broadcasted_iota(jnp.int32, (tile, head_dim), 1)
            state_ref[first_row : first_row + tile, :head_dim] = sums[:, :head_dim]
            state_ref[first_row : first_row + tile, head_dim:] = jnp.where(
                lane < head_dim // 2, sums[:, head_dim:], top
            )


def near_kernel(parts, sources, tile, block_rows, factor, start_ref, bias_ref, *refs):
    q_refs = refs[:parts]
    state_ref = refs[parts]
    k_refs = refs[parts + 1 : parts + 1 + sources]
    v_refs = refs[parts + 1 + sources : parts + 1 + 2 * sources]
    out_refs = refs[parts + 1 + 2 * sources :]
    rows, head_dim = q_refs[0].shape
    key_rows = jnp.concatenate([ref[...].reshape(-1, head_dim) for ref in k_refs], axis=0)
    value_rows = jnp.concatenate([ref[...].reshape(-1, head_dim) for ref in v_refs], axis=0)
    keys_marked = jnp.concatenate([key_rows, bias_ref[...]], axis=1)
    values_ones = jnp.concatenate([value_rows, jnp.ones_like(value_rows)], axis=1)
    for part in range(parts):
        for start in range(0, rows, tile):
            first_row = part * rows + start
            marked = query_rows(q_refs[part], start, first_row, tile, block_rows)
            scores = score_tile(marked, keys_marked)
            state = state_ref[first_row : first_row + tile, :]
            own_total = state[:, head_dim : head_dim + 1]
            own_top = state[:, 2 * head_dim - 1 :]
            top = jnp.maximum(jnp.max(scores, axis=1, keepdims=True), own_top)
            weights = jnp.exp2(scores * factor - top * factor).astype(jnp.bfloat16)
            sums = jnp.dot(weights, values_ones, preferred_element_type=jnp.float32)
            shrink = jnp.exp2(own_top * factor - top * factor)
            total = own_total * shrink + sums[:, head_dim : head_dim + 1]
            result = (state[:, :head_dim] * shrink + sums[:, :head_dim]) / total
            out_refs[part][start : start + tile, :] = result.astype(jnp.bfloat16)


def local(queries, keys, values, block_mask, strides, offsets):
    parts = lax.axis_size("head")
    frame_total = lax.axis_size("frame")
    here = lax.axis_index("head")
    frame_index = lax.axis_index("frame")
    rows, heads, head_dim = queries.shape
    frame_blocks = block_mask.shape[1]
    heads_here = heads // parts
    part_blocks = frame_blocks // parts
    block_rows = rows // part_blocks
    wide, narrow = frame_blocks // 4, frame_blocks // 2
    group_heads = min(2, heads_here)
    groups = heads_here // group_heads
    tile = min(256, rows)
    factor = head_dim ** (-0.5) * math.log2(math.e)
    early = part_blocks % narrow == 0

    packed = jnp.transpose(jnp.stack([keys, values, queries]), (0, 2, 1, 3))

    def head_slab(array, device, first, count):
        return lax.dynamic_slice_in_dim(array, device * heads_here + first, count, axis=1)

    part_ids = (here - jnp.arange(parts, dtype=jnp.int32)) % parts
    own_ids = (part_ids[:, None] * part_blocks + jnp.arange(part_blocks, dtype=jnp.int32)).reshape(-1)

    def slots(spacing):
        if early:
            inside = spacing * jnp.arange(part_blocks // spacing, dtype=jnp.int32)
            return (part_ids[:, None] * part_blocks + inside).reshape(-1)
        return spacing * jnp.arange(frame_blocks // spacing, dtype=jnp.int32)

    def firsts(spacing, frames):
        return (spacing - offsets[frames] % spacing) % spacing

    def exchange(slab_of):
        return [rotated(slab_of((here + s) % parts), "head", s) for s in range(1, parts)]

    my_wide = firsts(wide, frame_index)
    my_narrow = firsts(narrow, frame_index)
    my_anchor = firsts(frame_blocks, frame_index)
    if early:
        cut = packed[:2].reshape(2, heads, part_blocks // wide, wide, block_rows, head_dim)
        cut = lax.dynamic_index_in_dim(cut, my_wide, 3, keepdims=False)
        candidates = [head_slab(cut, here, 0, heads_here)]
        candidates += exchange(lambda device: head_slab(cut, device, 0, heads_here))
        candidates = jnp.stack(candidates, axis=2)

    arrived = []
    for group in range(groups):
        arrived.append(
            exchange(lambda device: head_slab(packed, device, group * group_heads, group_heads))
        )

    if early:
        wide_pack = candidates.reshape(2, heads_here, -1, head_dim)
        split = candidates.reshape(
            2, heads_here, parts * part_blocks // narrow, 2, block_rows, head_dim
        )
        narrow_pack = lax.dynamic_index_in_dim(split, my_narrow // wide, 3, keepdims=False)
        narrow_pack = narrow_pack.reshape(2, heads_here, -1, head_dim)
        anchor_part = (here - my_anchor // part_blocks) % parts
        anchor_spot = anchor_part * (part_blocks // wide) + (my_anchor % part_blocks) // wide
        anchor_pack = lax.dynamic_slice_in_dim(wide_pack, anchor_spot * block_rows, block_rows, axis=2)
    else:
        mine = head_slab(packed[:2], here, 0, heads_here)
        theirs = [
            jnp.concatenate([arrived[g][s][:2] for g in range(groups)], axis=1)
            for s in range(parts - 1)
        ]
        whole = jnp.stack([mine] + theirs, axis=2)
        whole = whole.reshape(2, heads_here, frame_blocks, block_rows, head_dim)

        def picked(ids):
            spots = (here - ids // part_blocks) % parts * part_blocks + ids % part_blocks
            return jnp.take(whole, spots, axis=2).reshape(2, heads_here, -1, head_dim)

        wide_pack = picked(my_wide + slots(wide))
        narrow_pack = picked(my_narrow + slots(narrow))
        anchor_pack = picked(my_anchor[None])

    gathered = lax.all_gather(anchor_pack, "frame", axis=0, tiled=False)
    sources = []
    id_lists, flag_lists = [own_ids], [jnp.ones((frame_blocks,), jnp.bool_)]
    for distance in (1, 2, 3):
        spacing = wide if distance == 1 else narrow
        for direction in (1, -1):
            pack = wide_pack if distance == 1 else narrow_pack
            sources.append(passed_along(pack, "frame", direction * distance))
            source = frame_index - direction * distance
            valid = (source >= 0) & (source < frame_total)
            clipped = jnp.clip(source, 0, frame_total - 1)
            chosen = firsts(spacing, clipped) + slots(spacing)
            id_lists.append(chosen)
            flag_lists.append(valid & ((chosen + offsets[clipped]) % strides[distance] == 0))
    frames = jnp.arange(frame_total, dtype=jnp.int32)
    spots = firsts(frame_blocks, frames)
    gaps = jnp.abs(frame_index - frames)
    id_lists.append(spots)
    flag_lists.append((gaps >= 4) & ((spots + offsets) % frame_blocks == 0))
    ids = jnp.concatenate(id_lists)
    flags = jnp.concatenate(flag_lists)

    own_mask = lax.dynamic_index_in_dim(block_mask, frame_index, 0, keepdims=False)
    kept = jnp.take(jnp.take(own_mask, own_ids, axis=0), ids, axis=1) == 1
    bias = jnp.where(kept & flags[None, :], 0.0, masked_score).astype(jnp.bfloat16).T
    bias = jnp.pad(bias, ((0, 0), (0, lanes - frame_blocks)))
    bias = jnp.repeat(bias, block_rows, axis=0)
    own_bias, near_bias = bias[: frame_blocks * block_rows], bias[frame_blocks * block_rows :]

    def scalar_grid(in_specs, out_specs):
        return pltpu.PrefetchScalarGridSpec(
            num_scalar_prefetch=1, grid=(group_heads,), in_specs=in_specs, out_specs=out_specs
        )

    def whole_block(array):
        return pl.BlockSpec(array.shape, lambda h, start: (0, 0))

    def own_block(which):
        return pl.BlockSpec(
            (None, None, rows, head_dim), lambda h, start: (which, start[0] + h, 0, 0)
        )

    def part_block(which):
        return pl.BlockSpec((None, None, rows, head_dim), lambda h, start: (which, h, 0, 0))

    params = pltpu.CompilerParams(vmem_limit_bytes=vmem_bytes)
    all_rows = parts * rows
    state_block = pl.BlockSpec((None, all_rows, 2 * head_dim), lambda h, start: (h, 0, 0))
    states, starts = [], []
    for group in range(groups):
        starts.append((here * heads_here + group * group_heads).reshape(1).astype(jnp.int32))
        blocks, operands = [], []
        for which in (2, 0, 1):
            blocks += [own_block(which)] + [part_block(which)] * (parts - 1)
            operands += [packed] + arrived[group]
        states.append(
            pl.pallas_call(
                functools.partial(own_kernel, parts, tile, block_rows, factor),
                grid_spec=scalar_grid([whole_block(own_bias)] + blocks, state_block),
                out_shape=jax.ShapeDtypeStruct(
                    (group_heads, all_rows, 2 * head_dim), jnp.float32
                ),
                compiler_params=params,
                cost_estimate=pl.CostEstimate(
                    flops=group_heads * 8 * all_rows * all_rows * head_dim,
                    bytes_accessed=group_heads * all_rows * head_dim * 14,
                    transcendentals=group_heads * all_rows * all_rows,
                ),
            )(starts[group], own_bias, *operands)
        )

    finished = []
    near_rows = near_bias.shape[0]
    for group in range(groups):
        base = group * group_heads

        def near_block(which, array):
            return pl.BlockSpec(
                (None, None) + array.shape[2:], lambda h, start: (which, base + h, 0, 0)
            )

        def anchor_block(which):
            return pl.BlockSpec(
                (frame_total, None, None, block_rows, head_dim),
                lambda h, start: (0, which, base + h, 0, 0),
            )

        blocks = [whole_block(near_bias), own_block(2)] + [part_block(2)] * (parts - 1)
        operands = [near_bias, packed] + arrived[group]
        blocks.append(state_block)
        operands.append(states[group])
        for which in (0, 1):
            blocks += [near_block(which, array) for array in sources] + [anchor_block(which)]
            operands += sources + [gathered]
        out_block = pl.BlockSpec((None, rows, head_dim), lambda h, start: (h, 0, 0))
        outs = pl.pallas_call(
            functools.partial(near_kernel, parts, len(sources) + 1, tile, block_rows, factor),
            grid_spec=scalar_grid(blocks, [out_block] * parts),
            out_shape=[jax.ShapeDtypeStruct((group_heads, rows, head_dim), jnp.bfloat16)] * parts,
            compiler_params=params,
            cost_estimate=pl.CostEstimate(
                flops=group_heads * 8 * all_rows * near_rows * head_dim,
                bytes_accessed=group_heads * (all_rows * 14 + near_rows * 4) * head_dim,
                transcendentals=group_heads * all_rows * near_rows,
            ),
        )(starts[group], *operands)
        finished.append([outs[0]] + [rotated(outs[p], "head", -p) for p in range(1, parts)])

    stacked = jnp.stack(
        [jnp.concatenate([entry[p] for entry in finished], axis=0) for p in range(parts)]
    )
    order = (jnp.arange(parts, dtype=jnp.int32) - here) % parts
    output = jnp.take(stacked, order, axis=0).reshape(heads, rows, head_dim)
    return jnp.transpose(output, (1, 0, 2))


def solution(mesh):
    placed = (
        P(("frame", "head"), None, None),
        P(("frame", "head"), None, None),
        P(("frame", "head"), None, None),
        P(),
        P(),
        P(),
    )
    return jax.shard_map(
        local,
        mesh=mesh,
        in_specs=placed,
        out_specs=P(("frame", "head"), None, None),
        check_vma=False,
    )
```

```python
import functools
import math

import jax
import jax.numpy as jnp
import numpy as np
from jax import lax
from jax.experimental import pallas as pl
from jax.experimental.pallas import tpu as pltpu
from jax.sharding import PartitionSpec as P

masked_score = -1e30
lanes = 128
vmem_bytes = 48 * 1024 * 1024


def rotated(block, axis, shift):
    size = lax.axis_size(axis)
    return lax.ppermute(block, axis, [(i, (i + shift) % size) for i in range(size)])


def passed_along(block, axis, distance):
    devices = range(lax.axis_size(axis))
    route = [(i - distance, i) for i in devices if i - distance in devices]
    return lax.ppermute(block, axis, route)


def query_rows(q_ref, start, first_row, tile, block_rows):
    query = q_ref[start : start + tile, :]
    row = lax.broadcasted_iota(jnp.int32, (tile, lanes), 0) + first_row
    lane = lax.broadcasted_iota(jnp.int32, (tile, lanes), 1)
    marks = jnp.where(row // block_rows == lane, 1.0, 0.0).astype(jnp.bfloat16)
    return jnp.concatenate([query, marks], axis=1)


def score_tile(query_marked, keys_marked):
    return lax.dot_general(
        query_marked, keys_marked, (((1,), (1,)), ((), ())), preferred_element_type=jnp.float32
    )


def own_kernel(parts, tile, block_rows, factor, start_ref, bias_ref, *refs):
    q_refs, k_refs, v_refs = refs[:parts], refs[parts : 2 * parts], refs[2 * parts : 3 * parts]
    state_ref = refs[3 * parts]
    key_rows = jnp.concatenate([ref[...] for ref in k_refs], axis=0)
    value_rows = jnp.concatenate([ref[...] for ref in v_refs], axis=0)
    keys_marked = jnp.concatenate([key_rows, bias_ref[...]], axis=1)
    values_ones = jnp.concatenate([value_rows, jnp.ones_like(value_rows)], axis=1)
    rows, head_dim = q_refs[0].shape
    for part in range(parts):
        for start in range(0, rows, tile):
            first_row = part * rows + start
            marked = query_rows(q_refs[part], start, first_row, tile, block_rows)
            scores = score_tile(marked, keys_marked)
            top = jnp.max(scores, axis=1, keepdims=True)
            weights = jnp.exp2(scores * factor - top * factor).astype(jnp.bfloat16)
            sums = jnp.dot(weights, values_ones, preferred_element_type=jnp.float32)
            lane = lax.broadcasted_iota(jnp.int32, (tile, head_dim), 1)
            state_ref[first_row : first_row + tile, :head_dim] = sums[:, :head_dim]
            state_ref[first_row : first_row + tile, head_dim:] = jnp.where(
                lane < head_dim // 2, sums[:, head_dim:], top
            )


def near_kernel(parts, sources, tile, block_rows, factor, start_ref, bias_ref, *refs):
    q_refs = refs[:parts]
    state_ref = refs[parts]
    k_refs = refs[parts + 1 : parts + 1 + sources]
    v_refs = refs[parts + 1 + sources : parts + 1 + 2 * sources]
    out_refs = refs[parts + 1 + 2 * sources :]
    rows, head_dim = q_refs[0].shape
    key_rows = jnp.concatenate([ref[...].reshape(-1, head_dim) for ref in k_refs], axis=0)
    value_rows = jnp.concatenate([ref[...].reshape(-1, head_dim) for ref in v_refs], axis=0)
    keys_marked = jnp.concatenate([key_rows, bias_ref[...]], axis=1)
    values_ones = jnp.concatenate([value_rows, jnp.ones_like(value_rows)], axis=1)
    for part in range(parts):
        for start in range(0, rows, tile):
            first_row = part * rows + start
            marked = query_rows(q_refs[part], start, first_row, tile, block_rows)
            scores = score_tile(marked, keys_marked)
            state = state_ref[first_row : first_row + tile, :]
            own_total = state[:, head_dim : head_dim + 1]
            own_top = state[:, 2 * head_dim - 1 :]
            top = jnp.maximum(jnp.max(scores, axis=1, keepdims=True), own_top)
            weights = jnp.exp2(scores * factor - top * factor).astype(jnp.bfloat16)
            sums = jnp.dot(weights, values_ones, preferred_element_type=jnp.float32)
            shrink = jnp.exp2(own_top * factor - top * factor)
            total = own_total * shrink + sums[:, head_dim : head_dim + 1]
            result = (state[:, :head_dim] * shrink + sums[:, :head_dim]) / total
            out_refs[part][start : start + tile, :] = result.astype(jnp.bfloat16)


def local(queries, keys, values, block_mask, strides, offsets):
    parts = lax.axis_size("head")
    frame_total = lax.axis_size("frame")
    here = lax.axis_index("head")
    frame_index = lax.axis_index("frame")
    rows, heads, head_dim = queries.shape
    frame_blocks = block_mask.shape[1]
    heads_here = heads // parts
    part_blocks = frame_blocks // parts
    block_rows = rows // part_blocks
    wide, narrow = frame_blocks // 4, frame_blocks // 2
    group_heads = min(2, heads_here)
    groups = heads_here // group_heads
    tile = min(256, rows)
    factor = head_dim ** (-0.5) * math.log2(math.e)
    early = part_blocks % narrow == 0

    packed = jnp.transpose(jnp.stack([keys, values, queries]), (0, 2, 1, 3))

    def head_slab(array, device, first, count):
        return lax.dynamic_slice_in_dim(array, device * heads_here + first, count, axis=1)

    part_ids = (here - jnp.arange(parts, dtype=jnp.int32)) % parts
    own_ids = (part_ids[:, None] * part_blocks + jnp.arange(part_blocks, dtype=jnp.int32)).reshape(-1)

    def slots(spacing):
        if early:
            inside = spacing * jnp.arange(part_blocks // spacing, dtype=jnp.int32)
            return (part_ids[:, None] * part_blocks + inside).reshape(-1)
        return spacing * jnp.arange(frame_blocks // spacing, dtype=jnp.int32)

    def firsts(spacing, frames):
        return (spacing - offsets[frames] % spacing) % spacing

    def exchange(slab_of):
        return [rotated(slab_of((here + s) % parts), "head", s) for s in range(1, parts)]

    my_wide = firsts(wide, frame_index)
    my_narrow = firsts(narrow, frame_index)
    my_anchor = firsts(frame_blocks, frame_index)
    if early:
        cut = packed[:2].reshape(2, heads, part_blocks // wide, wide, block_rows, head_dim)
        cut = lax.dynamic_index_in_dim(cut, my_wide, 3, keepdims=False)
        candidates = [head_slab(cut, here, 0, heads_here)]
        candidates += exchange(lambda device: head_slab(cut, device, 0, heads_here))
        candidates = jnp.stack(candidates, axis=2)

    arrived = []
    for group in range(groups):
        arrived.append(
            exchange(lambda device: head_slab(packed, device, group * group_heads, group_heads))
        )

    if early:
        wide_pack = candidates.reshape(2, heads_here, -1, head_dim)
        split = candidates.reshape(
            2, heads_here, parts * part_blocks // narrow, 2, block_rows, head_dim
        )
        narrow_pack = lax.dynamic_index_in_dim(split, my_narrow // wide, 3, keepdims=False)
        narrow_pack = narrow_pack.reshape(2, heads_here, -1, head_dim)
        anchor_part = (here - my_anchor // part_blocks) % parts
        anchor_spot = anchor_part * (part_blocks // wide) + (my_anchor % part_blocks) // wide
        anchor_pack = lax.dynamic_slice_in_dim(wide_pack, anchor_spot * block_rows, block_rows, axis=2)
    else:
        mine = head_slab(packed[:2], here, 0, heads_here)
        theirs = [
            jnp.concatenate([arrived[g][s][:2] for g in range(groups)], axis=1)
            for s in range(parts - 1)
        ]
        whole = jnp.stack([mine] + theirs, axis=2)
        whole = whole.reshape(2, heads_here, frame_blocks, block_rows, head_dim)

        def picked(ids):
            spots = (here - ids // part_blocks) % parts * part_blocks + ids % part_blocks
            return jnp.take(whole, spots, axis=2).reshape(2, heads_here, -1, head_dim)

        wide_pack = picked(my_wide + slots(wide))
        narrow_pack = picked(my_narrow + slots(narrow))
        anchor_pack = picked(my_anchor[None])

    gathered = lax.all_gather(anchor_pack, "frame", axis=0, tiled=False)
    sources = []
    id_lists, flag_lists = [own_ids], [jnp.ones((frame_blocks,), jnp.bool_)]
    for distance in (1, 2, 3):
        spacing = wide if distance == 1 else narrow
        for direction in (1, -1):
            pack = wide_pack if distance == 1 else narrow_pack
            sources.append(passed_along(pack, "frame", direction * distance))
            source = frame_index - direction * distance
            valid = (source >= 0) & (source < frame_total)
            clipped = jnp.clip(source, 0, frame_total - 1)
            chosen = firsts(spacing, clipped) + slots(spacing)
            id_lists.append(chosen)
            flag_lists.append(valid & ((chosen + offsets[clipped]) % strides[distance] == 0))
    frames = jnp.arange(frame_total, dtype=jnp.int32)
    spots = firsts(frame_blocks, frames)
    gaps = jnp.abs(frame_index - frames)
    id_lists.append(spots)
    flag_lists.append((gaps >= 4) & ((spots + offsets) % frame_blocks == 0))
    ids = jnp.concatenate(id_lists)
    flags = jnp.concatenate(flag_lists)

    own_mask = lax.dynamic_index_in_dim(block_mask, frame_index, 0, keepdims=False)
    kept = jnp.take(jnp.take(own_mask, own_ids, axis=0), ids, axis=1) == 1
    bias = jnp.where(kept & flags[None, :], 0.0, masked_score).astype(jnp.bfloat16).T
    bias = jnp.pad(bias, ((0, 0), (0, lanes - frame_blocks)))
    bias = jnp.repeat(bias, block_rows, axis=0)
    own_bias, near_bias = bias[: frame_blocks * block_rows], bias[frame_blocks * block_rows :]

    def scalar_grid(in_specs, out_specs):
        return pltpu.PrefetchScalarGridSpec(
            num_scalar_prefetch=1, grid=(group_heads,), in_specs=in_specs, out_specs=out_specs
        )

    def whole_block(array):
        return pl.BlockSpec(array.shape, lambda h, start: (0, 0))

    def own_block(which):
        return pl.BlockSpec(
            (None, None, rows, head_dim), lambda h, start: (which, start[0] + h, 0, 0)
        )

    def part_block(which):
        return pl.BlockSpec((None, None, rows, head_dim), lambda h, start: (which, h, 0, 0))

    params = pltpu.CompilerParams(vmem_limit_bytes=vmem_bytes)
    all_rows = parts * rows
    state_block = pl.BlockSpec((None, all_rows, 2 * head_dim), lambda h, start: (h, 0, 0))
    states, starts = [], []
    for group in range(groups):
        starts.append((here * heads_here + group * group_heads).reshape(1).astype(jnp.int32))
        blocks, operands = [], []
        for which in (2, 0, 1):
            blocks += [own_block(which)] + [part_block(which)] * (parts - 1)
            operands += [packed] + arrived[group]
        states.append(
            pl.pallas_call(
                functools.partial(own_kernel, parts, tile, block_rows, factor),
                grid_spec=scalar_grid([whole_block(own_bias)] + blocks, state_block),
                out_shape=jax.ShapeDtypeStruct(
                    (group_heads, all_rows, 2 * head_dim), jnp.float32
                ),
                compiler_params=params,
                cost_estimate=pl.CostEstimate(
                    flops=group_heads * 8 * all_rows * all_rows * head_dim,
                    bytes_accessed=group_heads * all_rows * head_dim * 14,
                    transcendentals=group_heads * all_rows * all_rows,
                ),
            )(starts[group], own_bias, *operands)
        )

    finished = []
    near_rows = near_bias.shape[0]
    for group in range(groups):
        base = group * group_heads

        def near_block(which, array):
            return pl.BlockSpec(
                (None, None) + array.shape[2:], lambda h, start: (which, base + h, 0, 0)
            )

        def anchor_block(which):
            return pl.BlockSpec(
                (frame_total, None, None, block_rows, head_dim),
                lambda h, start: (0, which, base + h, 0, 0),
            )

        blocks = [whole_block(near_bias), own_block(2)] + [part_block(2)] * (parts - 1)
        operands = [near_bias, packed] + arrived[group]
        blocks.append(state_block)
        operands.append(states[group])
        for which in (0, 1):
            blocks += [near_block(which, array) for array in sources] + [anchor_block(which)]
            operands += sources + [gathered]
        out_block = pl.BlockSpec((None, rows, head_dim), lambda h, start: (h, 0, 0))
        outs = pl.pallas_call(
            functools.partial(near_kernel, parts, len(sources) + 1, tile, block_rows, factor),
            grid_spec=scalar_grid(blocks, [out_block] * parts),
            out_shape=[jax.ShapeDtypeStruct((group_heads, rows, head_dim), jnp.bfloat16)] * parts,
            compiler_params=params,
            cost_estimate=pl.CostEstimate(
                flops=group_heads * 8 * all_rows * near_rows * head_dim,
                bytes_accessed=group_heads * (all_rows * 14 + near_rows * 4) * head_dim,
                transcendentals=group_heads * all_rows * near_rows,
            ),
        )(starts[group], *operands)
        finished.append([outs[0]] + [rotated(outs[p], "head", -p) for p in range(1, parts)])

    stacked = jnp.stack(
        [jnp.concatenate([entry[p] for entry in finished], axis=0) for p in range(parts)]
    )
    order = (jnp.arange(parts, dtype=jnp.int32) - here) % parts
    output = jnp.take(stacked, order, axis=0).reshape(heads, rows, head_dim)
    return jnp.transpose(output, (1, 0, 2))


def fused_kernel(
    groups, tile, factor, near_slots,
    bits_ref, mask_ref, q_ref, k_ref, v_ref, out_ref,
    kv, kv_in, q_in, wide_in, narrow_in, anchors, state, out_away, own_bias, near_bias,
    pair_send, pair_recv, near_send, near_recv, anchor_send, anchor_recv,
):
    here = lax.axis_index("head")
    frame = lax.axis_index("frame")
    frames = lax.axis_size("frame")
    other = 1 - here
    heads, rows, head_dim = q_ref.shape
    heads_here = heads // 2
    group_heads = heads_here // groups
    block_rows = wide_in.shape[5]
    part_blocks = rows // block_rows
    own_blocks = 2 * part_blocks
    all_rows = 2 * rows
    column, level = frame % 4, frame // 4

    def at_frame(target):
        return {"frame": target}

    level_two = (level + 2) % 4
    level_one = level + 1 - 2 * (level % 2)
    column_two = (column + 2) % 4
    column_one = column + 1 - 2 * (column % 2)
    hops = (
        level_two * 4 + column,
        level_one * 4 + column,
        level * 4 + column_two,
        level * 4 + column_one,
    )
    shifts = [(distance, sign) for distance in (1, 2, 3) for sign in (1, -1)]
    neighbours = [(frame + sign * distance + frames) % frames for distance, sign in shifts]

    barrier = pltpu.get_barrier_semaphore()
    pl.semaphore_signal(
        barrier, inc=1, device_id={"head": other}, device_id_type=pl.DeviceIdType.MESH
    )
    for target in list(hops) + neighbours:
        pl.semaphore_signal(
            barrier, inc=1, device_id=at_frame(target), device_id_type=pl.DeviceIdType.MESH
        )

    steps = part_blocks.bit_length() - 1
    turns = [bits_ref[step] == 1 for step in range(steps)]

    def turn_head(h, carry):
        for which, ref in ((0, k_ref), (1, v_ref)):
            blocks = [
                ref[h, slot * block_rows : (slot + 1) * block_rows, :]
                for slot in range(part_blocks)
            ]
            for step in range(steps):
                blocks = [
                    jnp.where(turns[step], blocks[(slot + 2**step) % part_blocks], blocks[slot])
                    for slot in range(part_blocks)
                ]
            for slot in range(part_blocks):
                place = (slot % (part_blocks // 2)) * block_rows
                half = slot // (part_blocks // 2)
                kv[which, h, half, place : place + block_rows, :] = blocks[slot]
        return carry

    lax.fori_loop(0, heads, turn_head, 0)
    pl.semaphore_wait(barrier, 1 + len(hops) + len(neighbours))

    def remote(src, dst, sends, recvs, index, device):
        return pltpu.make_async_remote_copy(
            src_ref=src,
            dst_ref=dst,
            send_sem=sends.at[index],
            recv_sem=recvs.at[index],
            device_id=device,
            device_id_type=pl.DeviceIdType.MESH,
        )

    pair = {"head": other}
    first = pl.ds(0, block_rows)
    rest = pl.ds(block_rows, rows // 2 - block_rows)
    mine = pl.ds(here * heads_here, heads_here)
    theirs = pl.ds(other * heads_here, heads_here)
    lead = remote(
        kv.at[:, theirs, :, first], kv_in.at[:, :, :, first], pair_send, pair_recv, 0, pair
    )
    lead.start()

    def near_copies(part):
        copies = []
        for index, (distance, sign) in enumerate(shifts):
            if distance == 1:
                src = kv.at[:, mine, :, first] if part == 0 else kv_in.at[:, :, :, first]
                dst = wide_in.at[index, part]
            else:
                src = kv.at[:, mine, 0, first] if part == 0 else kv_in.at[:, :, 0, first]
                dst = narrow_in.at[index - 2, part]
            copies.append(
                remote(
                    src, dst, near_send, near_recv, index * 2 + part, at_frame(neighbours[index])
                )
            )
        return copies

    near_first, near_second = near_copies(0), near_copies(1)
    group_copies = []
    for group in range(groups):
        away = pl.ds(other * heads_here + group * group_heads, group_heads)
        land = pl.ds(group * group_heads, group_heads)
        group_copies.append(
            [
                remote(
                    kv.at[:, away, :, rest], kv_in.at[:, land, :, rest],
                    pair_send, pair_recv, 1 + 2 * group, pair,
                ),
                remote(
                    q_ref.at[away], q_in.at[land], pair_send, pair_recv, 2 + 2 * group, pair
                ),
            ]
        )
    for copy in near_first:
        copy.start()
    for group in range(min(2, groups)):
        for copy in group_copies[group]:
            copy.start()

    def bias_rows(target, first_slot, count):
        for n in range(count):
            row = mask_ref[first_slot + n : first_slot + n + 1, :]
            target[n * block_rows : (n + 1) * block_rows, :] = jnp.broadcast_to(
                row, (block_rows, lanes)
            ).astype(jnp.bfloat16)

    bias_rows(own_bias, 0, own_blocks)
    bias_rows(near_bias, own_blocks, near_slots)

    lead.wait_recv()
    for copy in near_second:
        copy.start()
    from_here = bits_ref[steps] == 1
    for which in range(2):
        for h in range(heads_here):
            from_me = kv[which, here * heads_here + h, 0, :block_rows, :]
            from_pair = kv_in[which, h, 0, :block_rows, :]
            chosen = jnp.where(from_here, from_me, from_pair)
            anchors[column // 2, column % 2, level // 2, level % 2, which, h] = chosen
    spans = (
        anchors.at[column // 2, column % 2, level // 2, level % 2],
        anchors.at[column // 2, column % 2, :, level % 2],
        anchors.at[column // 2, column % 2],
        anchors.at[:, column % 2],
    )
    hop_copies = [
        remote(spans[hop], spans[hop], anchor_send, anchor_recv, hop, at_frame(hops[hop]))
        for hop in range(4)
    ]
    hop_copies[0].start()

    def query_tile(h, part, start):
        if part == 0:
            query = q_ref[here * heads_here + h, start : start + tile, :]
        else:
            query = q_in[h, start : start + tile, :]
        row = lax.broadcasted_iota(jnp.int32, (tile, lanes), 0) + (part * rows + start)
        lane = lax.broadcasted_iota(jnp.int32, (tile, lanes), 1) * block_rows
        inside = (row >= lane) & (row < lane + block_rows)
        marks = jnp.where(inside, 1.0, 0.0).astype(jnp.bfloat16)
        return jnp.concatenate([query, marks], axis=1)

    tiles = [(part, start) for part in range(2) for start in range(0, rows, tile)]

    def attend_own(h, carry):
        def both(which):
            return jnp.concatenate(
                [
                    kv[which, here * heads_here + h].reshape(rows, head_dim),
                    kv_in[which, h].reshape(rows, head_dim),
                ],
                axis=0,
            )

        keys_marked = jnp.concatenate([both(0), own_bias[...]], axis=1)
        value_rows = both(1)
        values_ones = jnp.concatenate([value_rows, jnp.ones_like(value_rows)], axis=1)
        for part, start in tiles:
            scores = score_tile(query_tile(h, part, start), keys_marked)
            top = jnp.max(scores, axis=1, keepdims=True)
            weights = jnp.exp2(scores * factor - top * factor).astype(jnp.bfloat16)
            sums = jnp.dot(weights, values_ones, preferred_element_type=jnp.float32)
            lane = lax.broadcasted_iota(jnp.int32, (tile, head_dim), 1)
            spot = part * rows + start
            state[h, spot : spot + tile, :head_dim] = sums[:, :head_dim]
            state[h, spot : spot + tile, head_dim:] = jnp.where(
                lane < head_dim // 2, sums[:, head_dim:], top
            )
        return carry

    def attend_near(h, carry):
        def all_sources(which):
            pieces = []
            for index in range(2):
                for part in range(2):
                    pieces.append(wide_in[index, part, which, h].reshape(-1, head_dim))
            for index in range(4):
                for part in range(2):
                    pieces.append(narrow_in[index, part, which, h])
            for gap in range(4, frames - 3):
                source = (frame + gap) % frames
                pieces.append(anchors[source % 4 // 2, source % 2, source // 8, source // 4 % 2, which, h])
            return jnp.concatenate(pieces, axis=0)

        keys_marked = jnp.concatenate([all_sources(0), near_bias[...]], axis=1)
        value_rows = all_sources(1)
        values_ones = jnp.concatenate([value_rows, jnp.ones_like(value_rows)], axis=1)
        for part, start in tiles:
            scores = score_tile(query_tile(h, part, start), keys_marked)
            spot = part * rows + start
            own_sums = state[h, spot : spot + tile, :head_dim]
            own_rest = state[h, spot : spot + tile, head_dim:]
            own_total, own_top = own_rest[:, :1], own_rest[:, head_dim - 1 :]
            top = jnp.maximum(jnp.max(scores, axis=1, keepdims=True), own_top)
            weights = jnp.exp2(scores * factor - top * factor).astype(jnp.bfloat16)
            sums = jnp.dot(weights, values_ones, preferred_element_type=jnp.float32)
            shrink = jnp.exp2(own_top * factor - top * factor)
            total = own_total * shrink + sums[:, head_dim : head_dim + 1]
            result = (own_sums * shrink + sums[:, :head_dim]) / total
            if part == 0:
                out_ref[here * heads_here + h, start : start + tile, :] = result.astype(jnp.bfloat16)
            else:
                out_away[h, start : start + tile, :] = result.astype(jnp.bfloat16)
        return carry

    returns = []

    def own_step(group):
        for copy in group_copies[group]:
            copy.wait_recv()
        if group + 2 < groups:
            for copy in group_copies[group + 2]:
                copy.start()
        lax.fori_loop(group * group_heads, (group + 1) * group_heads, attend_own, 0)

    def near_step(group):
        lax.fori_loop(group * group_heads, (group + 1) * group_heads, attend_near, 0)
        copy = remote(
            out_away.at[pl.ds(group * group_heads, group_heads)],
            out_ref.at[pl.ds(here * heads_here + group * group_heads, group_heads)],
            pair_send, pair_recv, 1 + 2 * groups + group, pair,
        )
        copy.start()
        returns.append(copy)

    own_step(0)
    hop_copies[0].wait_recv()
    hop_copies[1].start()
    own_step(1)
    hop_copies[1].wait_recv()
    hop_copies[2].start()
    own_step(2)
    hop_copies[2].wait_recv()
    hop_copies[3].start()
    for copy in near_first + near_second:
        copy.wait_recv()
    hop_copies[3].wait_recv()
    near_step(0)
    near_step(1)
    own_step(3)
    near_step(2)
    near_step(3)
    lead.wait_send()
    for copy in near_first + near_second + hop_copies:
        copy.wait_send()
    for copies in group_copies:
        for copy in copies:
            copy.wait_send()
    for copy in returns:
        copy.wait()


def local_pair(queries, keys, values, block_mask, strides, offsets):
    frames = lax.axis_size("frame")
    here = lax.axis_index("head")
    frame = lax.axis_index("frame")
    rows, heads, head_dim = queries.shape
    frame_blocks = block_mask.shape[1]
    part_blocks = frame_blocks // 2
    block_rows = rows // part_blocks
    heads_here = heads // 2
    groups = 4
    wide, narrow = frame_blocks // 4, frame_blocks // 2
    factor = head_dim ** (-0.5) * math.log2(math.e)

    table = [(0, half, slot, 0) for half in range(2) for slot in range(part_blocks)]
    for distance in (1, 2, 3):
        for sign in (1, -1):
            for half in range(2):
                for slot in [0, wide] if distance == 1 else [0]:
                    table.append((-sign * distance, half, slot, distance))
    table += [(gap, 0, 0, frames) for gap in range(4, frames - 3)]
    shift, half, slot, kind = (jnp.asarray(column, jnp.int32) for column in np.array(table).T)
    near_slots = len(table) - frame_blocks
    frame_ids = jnp.arange(frames, dtype=jnp.int32)

    def looked_up(array, index):
        return jnp.sum(jnp.where(index[:, None] == frame_ids[None, :], array[None, :], 0), axis=1)

    source = lax.rem(frame + shift + frames, frames)
    phase = looked_up(offsets, source)
    turn = lax.rem(narrow - lax.rem(phase, narrow), narrow)
    anchor = lax.rem(frame_blocks - lax.rem(phase, frame_blocks), frame_blocks)
    part = jnp.where(half == 0, here, 1 - here)
    ids = jnp.where(kind == frames, anchor, part * part_blocks + lax.rem(turn + slot, part_blocks))
    gap = jnp.abs(frame - source)
    spacing = jnp.where(gap == kind, looked_up(strides, gap), frame_blocks)
    flags = (kind == 0) | (lax.rem(ids + phase, spacing) == 0)
    steps = part_blocks.bit_length() - 1
    powers = jnp.asarray([2**step for step in range(steps)] + [0], jnp.int32)
    bits = jnp.where(
        powers > 0,
        lax.rem(turn[0] // jnp.maximum(powers, 1), 2),
        (anchor[0] // part_blocks == here).astype(jnp.int32),
    )

    own_mask = lax.dynamic_index_in_dim(block_mask, frame, 0, keepdims=False)
    swapped = jnp.concatenate([own_mask[part_blocks:], own_mask[:part_blocks]], axis=0)
    own_mask = jnp.where(here == 0, own_mask, swapped)
    block_ids = jnp.arange(frame_blocks, dtype=jnp.int32)
    picks = ids[:, None, None] == block_ids[None, None, :]
    kept = jnp.sum(jnp.where(picks, own_mask[None, :, :], 0), axis=2) == 1
    mask = jnp.where(kept & flags[:, None], 0.0, masked_score).astype(jnp.float32)
    mask = jnp.pad(mask, ((0, 0), (0, lanes - frame_blocks)))

    bf16 = jnp.bfloat16
    near_rows = near_slots * block_rows
    all_rows = 2 * rows
    vmem = pl.BlockSpec(memory_space=pltpu.VMEM)
    smem = pl.BlockSpec(memory_space=pltpu.SMEM)
    pair_count = 1 + 3 * groups
    dma = pltpu.SemaphoreType.DMA
    total_rows = all_rows + near_rows
    output = pl.pallas_call(
        functools.partial(fused_kernel, groups, min(256, rows), factor, near_slots),
        out_shape=jax.ShapeDtypeStruct((heads, rows, head_dim), bf16),
        in_specs=[smem, vmem, vmem, vmem, vmem],
        out_specs=vmem,
        scratch_shapes=[
            pltpu.VMEM((2, heads, 2, rows // 2, head_dim), bf16),
            pltpu.VMEM((2, heads_here, 2, rows // 2, head_dim), bf16),
            pltpu.VMEM((heads_here, rows, head_dim), bf16),
            pltpu.VMEM((2, 2, 2, heads_here, 2, block_rows, head_dim), bf16),
            pltpu.VMEM((4, 2, 2, heads_here, block_rows, head_dim), bf16),
            pltpu.VMEM((2, 2, 2, 2, 2, heads_here, block_rows, head_dim), bf16),
            pltpu.VMEM((heads_here, all_rows, 2 * head_dim), jnp.float32),
            pltpu.VMEM((heads_here, rows, head_dim), bf16),
            pltpu.VMEM((all_rows, lanes), bf16),
            pltpu.VMEM((near_rows, lanes), bf16),
            dma((pair_count,)),
            dma((pair_count,)),
            dma((12,)),
            dma((12,)),
            dma((4,)),
            dma((4,)),
        ],
        compiler_params=pltpu.CompilerParams(
            collective_id=0, has_side_effects=True, vmem_limit_bytes=56 * 1024 * 1024
        ),
        cost_estimate=pl.CostEstimate(
            flops=heads_here * 8 * all_rows * total_rows * head_dim,
            bytes_accessed=8 * heads * rows * head_dim,
            transcendentals=heads_here * all_rows * total_rows,
        ),
    )(
        bits,
        mask,
        jnp.transpose(queries, (1, 0, 2)),
        jnp.transpose(keys, (1, 0, 2)),
        jnp.transpose(values, (1, 0, 2)),
    )
    return jnp.transpose(output, (1, 0, 2))


def solution(mesh):
    paired = mesh.shape["head"] == 2 and mesh.shape["frame"] == 16
    placed = (
        P(("frame", "head"), None, None),
        P(("frame", "head"), None, None),
        P(("frame", "head"), None, None),
        P(),
        P(),
        P(),
    )
    return jax.shard_map(
        local_pair if paired else local,
        mesh=mesh,
        in_specs=placed,
        out_specs=P(("frame", "head"), None, None),
        check_vma=False,
    )
```

```python
import functools
import math

import jax
import jax.numpy as jnp
import numpy as np
from jax import lax
from jax.experimental import pallas as pl
from jax.experimental.pallas import tpu as pltpu
from jax.sharding import PartitionSpec as P

masked_score = -1e30
lanes = 128
vmem_bytes = 48 * 1024 * 1024


def rotated(block, axis, shift):
    size = lax.axis_size(axis)
    return lax.ppermute(block, axis, [(i, (i + shift) % size) for i in range(size)])


def passed_along(block, axis, distance):
    devices = range(lax.axis_size(axis))
    route = [(i - distance, i) for i in devices if i - distance in devices]
    return lax.ppermute(block, axis, route)


def query_rows(q_ref, start, first_row, tile, block_rows):
    query = q_ref[start : start + tile, :]
    row = lax.broadcasted_iota(jnp.int32, (tile, lanes), 0) + first_row
    lane = lax.broadcasted_iota(jnp.int32, (tile, lanes), 1)
    marks = jnp.where(row // block_rows == lane, 1.0, 0.0).astype(jnp.bfloat16)
    return jnp.concatenate([query, marks], axis=1)


def score_tile(query_marked, keys_marked):
    return lax.dot_general(
        query_marked, keys_marked, (((1,), (1,)), ((), ())), preferred_element_type=jnp.float32
    )


def own_kernel(parts, tile, block_rows, factor, start_ref, bias_ref, *refs):
    q_refs, k_refs, v_refs = refs[:parts], refs[parts : 2 * parts], refs[2 * parts : 3 * parts]
    state_ref = refs[3 * parts]
    key_rows = jnp.concatenate([ref[...] for ref in k_refs], axis=0)
    value_rows = jnp.concatenate([ref[...] for ref in v_refs], axis=0)
    keys_marked = jnp.concatenate([key_rows, bias_ref[...]], axis=1)
    values_ones = jnp.concatenate([value_rows, jnp.ones_like(value_rows)], axis=1)
    rows, head_dim = q_refs[0].shape
    for part in range(parts):
        for start in range(0, rows, tile):
            first_row = part * rows + start
            marked = query_rows(q_refs[part], start, first_row, tile, block_rows)
            scores = score_tile(marked, keys_marked)
            top = jnp.max(scores, axis=1, keepdims=True)
            weights = jnp.exp2(scores * factor - top * factor).astype(jnp.bfloat16)
            sums = jnp.dot(weights, values_ones, preferred_element_type=jnp.float32)
            lane = lax.broadcasted_iota(jnp.int32, (tile, head_dim), 1)
            state_ref[first_row : first_row + tile, :head_dim] = sums[:, :head_dim]
            state_ref[first_row : first_row + tile, head_dim:] = jnp.where(
                lane < head_dim // 2, sums[:, head_dim:], top
            )


def near_kernel(parts, sources, tile, block_rows, factor, start_ref, bias_ref, *refs):
    q_refs = refs[:parts]
    state_ref = refs[parts]
    k_refs = refs[parts + 1 : parts + 1 + sources]
    v_refs = refs[parts + 1 + sources : parts + 1 + 2 * sources]
    out_refs = refs[parts + 1 + 2 * sources :]
    rows, head_dim = q_refs[0].shape
    key_rows = jnp.concatenate([ref[...].reshape(-1, head_dim) for ref in k_refs], axis=0)
    value_rows = jnp.concatenate([ref[...].reshape(-1, head_dim) for ref in v_refs], axis=0)
    keys_marked = jnp.concatenate([key_rows, bias_ref[...]], axis=1)
    values_ones = jnp.concatenate([value_rows, jnp.ones_like(value_rows)], axis=1)
    for part in range(parts):
        for start in range(0, rows, tile):
            first_row = part * rows + start
            marked = query_rows(q_refs[part], start, first_row, tile, block_rows)
            scores = score_tile(marked, keys_marked)
            state = state_ref[first_row : first_row + tile, :]
            own_total = state[:, head_dim : head_dim + 1]
            own_top = state[:, 2 * head_dim - 1 :]
            top = jnp.maximum(jnp.max(scores, axis=1, keepdims=True), own_top)
            weights = jnp.exp2(scores * factor - top * factor).astype(jnp.bfloat16)
            sums = jnp.dot(weights, values_ones, preferred_element_type=jnp.float32)
            shrink = jnp.exp2(own_top * factor - top * factor)
            total = own_total * shrink + sums[:, head_dim : head_dim + 1]
            result = (state[:, :head_dim] * shrink + sums[:, :head_dim]) / total
            out_refs[part][start : start + tile, :] = result.astype(jnp.bfloat16)


def local(queries, keys, values, block_mask, strides, offsets):
    parts = lax.axis_size("head")
    frame_total = lax.axis_size("frame")
    here = lax.axis_index("head")
    frame_index = lax.axis_index("frame")
    rows, heads, head_dim = queries.shape
    frame_blocks = block_mask.shape[1]
    heads_here = heads // parts
    part_blocks = frame_blocks // parts
    block_rows = rows // part_blocks
    wide, narrow = frame_blocks // 4, frame_blocks // 2
    group_heads = min(2, heads_here)
    groups = heads_here // group_heads
    tile = min(256, rows)
    factor = head_dim ** (-0.5) * math.log2(math.e)
    early = part_blocks % narrow == 0

    packed = jnp.transpose(jnp.stack([keys, values, queries]), (0, 2, 1, 3))

    def head_slab(array, device, first, count):
        return lax.dynamic_slice_in_dim(array, device * heads_here + first, count, axis=1)

    part_ids = (here - jnp.arange(parts, dtype=jnp.int32)) % parts
    own_ids = (part_ids[:, None] * part_blocks + jnp.arange(part_blocks, dtype=jnp.int32)).reshape(-1)

    def slots(spacing):
        if early:
            inside = spacing * jnp.arange(part_blocks // spacing, dtype=jnp.int32)
            return (part_ids[:, None] * part_blocks + inside).reshape(-1)
        return spacing * jnp.arange(frame_blocks // spacing, dtype=jnp.int32)

    def firsts(spacing, frames):
        return (spacing - offsets[frames] % spacing) % spacing

    def exchange(slab_of):
        return [rotated(slab_of((here + s) % parts), "head", s) for s in range(1, parts)]

    my_wide = firsts(wide, frame_index)
    my_narrow = firsts(narrow, frame_index)
    my_anchor = firsts(frame_blocks, frame_index)
    if early:
        cut = packed[:2].reshape(2, heads, part_blocks // wide, wide, block_rows, head_dim)
        cut = lax.dynamic_index_in_dim(cut, my_wide, 3, keepdims=False)
        candidates = [head_slab(cut, here, 0, heads_here)]
        candidates += exchange(lambda device: head_slab(cut, device, 0, heads_here))
        candidates = jnp.stack(candidates, axis=2)

    arrived = []
    for group in range(groups):
        arrived.append(
            exchange(lambda device: head_slab(packed, device, group * group_heads, group_heads))
        )

    if early:
        wide_pack = candidates.reshape(2, heads_here, -1, head_dim)
        split = candidates.reshape(
            2, heads_here, parts * part_blocks // narrow, 2, block_rows, head_dim
        )
        narrow_pack = lax.dynamic_index_in_dim(split, my_narrow // wide, 3, keepdims=False)
        narrow_pack = narrow_pack.reshape(2, heads_here, -1, head_dim)
        anchor_part = (here - my_anchor // part_blocks) % parts
        anchor_spot = anchor_part * (part_blocks // wide) + (my_anchor % part_blocks) // wide
        anchor_pack = lax.dynamic_slice_in_dim(wide_pack, anchor_spot * block_rows, block_rows, axis=2)
    else:
        mine = head_slab(packed[:2], here, 0, heads_here)
        theirs = [
            jnp.concatenate([arrived[g][s][:2] for g in range(groups)], axis=1)
            for s in range(parts - 1)
        ]
        whole = jnp.stack([mine] + theirs, axis=2)
        whole = whole.reshape(2, heads_here, frame_blocks, block_rows, head_dim)

        def picked(ids):
            spots = (here - ids // part_blocks) % parts * part_blocks + ids % part_blocks
            return jnp.take(whole, spots, axis=2).reshape(2, heads_here, -1, head_dim)

        wide_pack = picked(my_wide + slots(wide))
        narrow_pack = picked(my_narrow + slots(narrow))
        anchor_pack = picked(my_anchor[None])

    gathered = lax.all_gather(anchor_pack, "frame", axis=0, tiled=False)
    sources = []
    id_lists, flag_lists = [own_ids], [jnp.ones((frame_blocks,), jnp.bool_)]
    for distance in (1, 2, 3):
        spacing = wide if distance == 1 else narrow
        for direction in (1, -1):
            pack = wide_pack if distance == 1 else narrow_pack
            sources.append(passed_along(pack, "frame", direction * distance))
            source = frame_index - direction * distance
            valid = (source >= 0) & (source < frame_total)
            clipped = jnp.clip(source, 0, frame_total - 1)
            chosen = firsts(spacing, clipped) + slots(spacing)
            id_lists.append(chosen)
            flag_lists.append(valid & ((chosen + offsets[clipped]) % strides[distance] == 0))
    frames = jnp.arange(frame_total, dtype=jnp.int32)
    spots = firsts(frame_blocks, frames)
    gaps = jnp.abs(frame_index - frames)
    id_lists.append(spots)
    flag_lists.append((gaps >= 4) & ((spots + offsets) % frame_blocks == 0))
    ids = jnp.concatenate(id_lists)
    flags = jnp.concatenate(flag_lists)

    own_mask = lax.dynamic_index_in_dim(block_mask, frame_index, 0, keepdims=False)
    kept = jnp.take(jnp.take(own_mask, own_ids, axis=0), ids, axis=1) == 1
    bias = jnp.where(kept & flags[None, :], 0.0, masked_score).astype(jnp.bfloat16).T
    bias = jnp.pad(bias, ((0, 0), (0, lanes - frame_blocks)))
    bias = jnp.repeat(bias, block_rows, axis=0)
    own_bias, near_bias = bias[: frame_blocks * block_rows], bias[frame_blocks * block_rows :]

    def scalar_grid(in_specs, out_specs):
        return pltpu.PrefetchScalarGridSpec(
            num_scalar_prefetch=1, grid=(group_heads,), in_specs=in_specs, out_specs=out_specs
        )

    def whole_block(array):
        return pl.BlockSpec(array.shape, lambda h, start: (0, 0))

    def own_block(which):
        return pl.BlockSpec(
            (None, None, rows, head_dim), lambda h, start: (which, start[0] + h, 0, 0)
        )

    def part_block(which):
        return pl.BlockSpec((None, None, rows, head_dim), lambda h, start: (which, h, 0, 0))

    params = pltpu.CompilerParams(vmem_limit_bytes=vmem_bytes)
    all_rows = parts * rows
    state_block = pl.BlockSpec((None, all_rows, 2 * head_dim), lambda h, start: (h, 0, 0))
    states, starts = [], []
    for group in range(groups):
        starts.append((here * heads_here + group * group_heads).reshape(1).astype(jnp.int32))
        blocks, operands = [], []
        for which in (2, 0, 1):
            blocks += [own_block(which)] + [part_block(which)] * (parts - 1)
            operands += [packed] + arrived[group]
        states.append(
            pl.pallas_call(
                functools.partial(own_kernel, parts, tile, block_rows, factor),
                grid_spec=scalar_grid([whole_block(own_bias)] + blocks, state_block),
                out_shape=jax.ShapeDtypeStruct(
                    (group_heads, all_rows, 2 * head_dim), jnp.float32
                ),
                compiler_params=params,
                cost_estimate=pl.CostEstimate(
                    flops=group_heads * 8 * all_rows * all_rows * head_dim,
                    bytes_accessed=group_heads * all_rows * head_dim * 14,
                    transcendentals=group_heads * all_rows * all_rows,
                ),
            )(starts[group], own_bias, *operands)
        )

    finished = []
    near_rows = near_bias.shape[0]
    for group in range(groups):
        base = group * group_heads

        def near_block(which, array):
            return pl.BlockSpec(
                (None, None) + array.shape[2:], lambda h, start: (which, base + h, 0, 0)
            )

        def anchor_block(which):
            return pl.BlockSpec(
                (frame_total, None, None, block_rows, head_dim),
                lambda h, start: (0, which, base + h, 0, 0),
            )

        blocks = [whole_block(near_bias), own_block(2)] + [part_block(2)] * (parts - 1)
        operands = [near_bias, packed] + arrived[group]
        blocks.append(state_block)
        operands.append(states[group])
        for which in (0, 1):
            blocks += [near_block(which, array) for array in sources] + [anchor_block(which)]
            operands += sources + [gathered]
        out_block = pl.BlockSpec((None, rows, head_dim), lambda h, start: (h, 0, 0))
        outs = pl.pallas_call(
            functools.partial(near_kernel, parts, len(sources) + 1, tile, block_rows, factor),
            grid_spec=scalar_grid(blocks, [out_block] * parts),
            out_shape=[jax.ShapeDtypeStruct((group_heads, rows, head_dim), jnp.bfloat16)] * parts,
            compiler_params=params,
            cost_estimate=pl.CostEstimate(
                flops=group_heads * 8 * all_rows * near_rows * head_dim,
                bytes_accessed=group_heads * (all_rows * 14 + near_rows * 4) * head_dim,
                transcendentals=group_heads * all_rows * near_rows,
            ),
        )(starts[group], *operands)
        finished.append([outs[0]] + [rotated(outs[p], "head", -p) for p in range(1, parts)])

    stacked = jnp.stack(
        [jnp.concatenate([entry[p] for entry in finished], axis=0) for p in range(parts)]
    )
    order = (jnp.arange(parts, dtype=jnp.int32) - here) % parts
    output = jnp.take(stacked, order, axis=0).reshape(heads, rows, head_dim)
    return jnp.transpose(output, (1, 0, 2))


def fused_kernel(
    groups, tile, factor, near_slots,
    bits_ref, mask_ref, q_ref, k_ref, v_ref, out_ref,
    kv, kv_in, q_in, wide_in, narrow_in, anchors, state, out_away, own_bias, near_bias,
    pair_send, pair_recv, near_send, near_recv, anchor_send, anchor_recv,
):
    here = lax.axis_index("head")
    frame = lax.axis_index("frame")
    frames = lax.axis_size("frame")
    other = 1 - here
    heads, rows, head_dim = q_ref.shape
    heads_here = heads // 2
    group_heads = heads_here // groups
    block_rows = wide_in.shape[5]
    part_blocks = rows // block_rows
    own_blocks = 2 * part_blocks
    all_rows = 2 * rows
    column, level = frame % 4, frame // 4

    def at_frame(target):
        return {"frame": target}

    level_two = (level + 2) % 4
    level_one = level + 1 - 2 * (level % 2)
    column_two = (column + 2) % 4
    column_one = column + 1 - 2 * (column % 2)
    hops = (
        level_two * 4 + column,
        level_one * 4 + column,
        level * 4 + column_two,
        level * 4 + column_one,
    )
    shifts = [(distance, sign) for distance in (1, 2, 3) for sign in (1, -1)]
    neighbours = [(frame + sign * distance + frames) % frames for distance, sign in shifts]

    barrier = pltpu.get_barrier_semaphore()
    pl.semaphore_signal(
        barrier, inc=1, device_id={"head": other}, device_id_type=pl.DeviceIdType.MESH
    )
    for target in list(hops) + neighbours:
        pl.semaphore_signal(
            barrier, inc=1, device_id=at_frame(target), device_id_type=pl.DeviceIdType.MESH
        )

    steps = part_blocks.bit_length() - 1
    turns = [bits_ref[step] == 1 for step in range(steps)]

    def turn_head(h, carry):
        for which, ref in ((0, k_ref), (1, v_ref)):
            blocks = [
                ref[h, slot * block_rows : (slot + 1) * block_rows, :]
                for slot in range(part_blocks)
            ]
            for step in range(steps):
                blocks = [
                    jnp.where(turns[step], blocks[(slot + 2**step) % part_blocks], blocks[slot])
                    for slot in range(part_blocks)
                ]
            for slot in range(part_blocks):
                place = (slot % (part_blocks // 2)) * block_rows
                half = slot // (part_blocks // 2)
                kv[which, h, half, place : place + block_rows, :] = blocks[slot]
        return carry

    lax.fori_loop(0, heads, turn_head, 0)
    pl.semaphore_wait(barrier, 1 + len(hops) + len(neighbours))

    def remote(src, dst, sends, recvs, index, device):
        return pltpu.make_async_remote_copy(
            src_ref=src,
            dst_ref=dst,
            send_sem=sends.at[index],
            recv_sem=recvs.at[index],
            device_id=device,
            device_id_type=pl.DeviceIdType.MESH,
        )

    pair = {"head": other}
    first = pl.ds(0, block_rows)
    rest = pl.ds(block_rows, rows // 2 - block_rows)
    mine = pl.ds(here * heads_here, heads_here)
    theirs = pl.ds(other * heads_here, heads_here)
    lead = remote(
        kv.at[:, theirs, :, first], kv_in.at[:, :, :, first], pair_send, pair_recv, 0, pair
    )
    lead.start()

    def near_copies(part):
        copies = []
        for index, (distance, sign) in enumerate(shifts):
            if distance == 1:
                src = kv.at[:, mine, :, first] if part == 0 else kv_in.at[:, :, :, first]
                dst = wide_in.at[index, part]
            else:
                src = kv.at[:, mine, 0, first] if part == 0 else kv_in.at[:, :, 0, first]
                dst = narrow_in.at[index - 2, part]
            copies.append(
                remote(
                    src, dst, near_send, near_recv, index * 2 + part, at_frame(neighbours[index])
                )
            )
        return copies

    near_first, near_second = near_copies(0), near_copies(1)
    group_copies = []
    for group in range(groups):
        away = pl.ds(other * heads_here + group * group_heads, group_heads)
        land = pl.ds(group * group_heads, group_heads)
        group_copies.append(
            [
                remote(
                    kv.at[:, away, :, rest], kv_in.at[:, land, :, rest],
                    pair_send, pair_recv, 1 + 2 * group, pair,
                ),
                remote(
                    q_ref.at[away], q_in.at[land], pair_send, pair_recv, 2 + 2 * group, pair
                ),
            ]
        )
    for copy in near_first:
        copy.start()
    for group in range(min(2, groups)):
        for copy in group_copies[group]:
            copy.start()

    def bias_rows(target, first_slot, count):
        for n in range(count):
            row = mask_ref[first_slot + n : first_slot + n + 1, :]
            target[n * block_rows : (n + 1) * block_rows, :] = jnp.broadcast_to(
                row, (block_rows, lanes)
            ).astype(jnp.bfloat16)

    bias_rows(own_bias, 0, own_blocks)
    bias_rows(near_bias, own_blocks, near_slots)

    lead.wait_recv()
    for copy in near_second:
        copy.start()
    from_here = bits_ref[steps] == 1
    for which in range(2):
        for h in range(heads_here):
            from_me = kv[which, here * heads_here + h, 0, :block_rows, :]
            from_pair = kv_in[which, h, 0, :block_rows, :]
            chosen = jnp.where(from_here, from_me, from_pair)
            anchors[column // 2, column % 2, level // 2, level % 2, which, h] = chosen
    spans = (
        anchors.at[column // 2, column % 2, level // 2, level % 2],
        anchors.at[column // 2, column % 2, :, level % 2],
        anchors.at[column // 2, column % 2],
        anchors.at[:, column % 2],
    )
    hop_copies = [
        remote(spans[hop], spans[hop], anchor_send, anchor_recv, hop, at_frame(hops[hop]))
        for hop in range(4)
    ]
    hop_copies[0].start()

    def query_tile(h, part, start):
        if part == 0:
            query = q_ref[here * heads_here + h, start : start + tile, :]
        else:
            query = q_in[h, start : start + tile, :]
        row = lax.broadcasted_iota(jnp.int32, (tile, lanes), 0) + (part * rows + start)
        lane = lax.broadcasted_iota(jnp.int32, (tile, lanes), 1) * block_rows
        inside = (row >= lane) & (row < lane + block_rows)
        marks = jnp.where(inside, 1.0, 0.0).astype(jnp.bfloat16)
        return jnp.concatenate([query, marks], axis=1)

    tiles = [(part, start) for part in range(2) for start in range(0, rows, tile)]

    def attend_own(h, carry):
        def both(which):
            return jnp.concatenate(
                [
                    kv[which, here * heads_here + h].reshape(rows, head_dim),
                    kv_in[which, h].reshape(rows, head_dim),
                ],
                axis=0,
            )

        keys_marked = jnp.concatenate([both(0), own_bias[...]], axis=1)
        value_rows = both(1)
        values_ones = jnp.concatenate([value_rows, jnp.ones_like(value_rows)], axis=1)
        for part, start in tiles:
            scores = score_tile(query_tile(h, part, start), keys_marked)
            top = jnp.max(scores, axis=1, keepdims=True)
            weights = jnp.exp2(scores * factor - top * factor).astype(jnp.bfloat16)
            sums = jnp.dot(weights, values_ones, preferred_element_type=jnp.float32)
            lane = lax.broadcasted_iota(jnp.int32, (tile, head_dim), 1)
            spot = part * rows + start
            state[h, spot : spot + tile, :head_dim] = sums[:, :head_dim]
            state[h, spot : spot + tile, head_dim:] = jnp.where(
                lane < head_dim // 2, sums[:, head_dim:], top
            )
        return carry

    def attend_near(h, carry):
        def all_sources(which):
            pieces = []
            for index in range(2):
                for part in range(2):
                    pieces.append(wide_in[index, part, which, h].reshape(-1, head_dim))
            for index in range(4):
                for part in range(2):
                    pieces.append(narrow_in[index, part, which, h])
            for gap in range(4, frames - 3):
                source = (frame + gap) % frames
                pieces.append(anchors[source % 4 // 2, source % 2, source // 8, source // 4 % 2, which, h])
            return jnp.concatenate(pieces, axis=0)

        keys_marked = jnp.concatenate([all_sources(0), near_bias[...]], axis=1)
        value_rows = all_sources(1)
        values_ones = jnp.concatenate([value_rows, jnp.ones_like(value_rows)], axis=1)
        for part, start in tiles:
            scores = score_tile(query_tile(h, part, start), keys_marked)
            spot = part * rows + start
            own_sums = state[h, spot : spot + tile, :head_dim]
            own_rest = state[h, spot : spot + tile, head_dim:]
            own_total, own_top = own_rest[:, :1], own_rest[:, head_dim - 1 :]
            top = jnp.maximum(jnp.max(scores, axis=1, keepdims=True), own_top)
            weights = jnp.exp2(scores * factor - top * factor).astype(jnp.bfloat16)
            sums = jnp.dot(weights, values_ones, preferred_element_type=jnp.float32)
            shrink = jnp.exp2(own_top * factor - top * factor)
            total = own_total * shrink + sums[:, head_dim : head_dim + 1]
            result = (own_sums * shrink + sums[:, :head_dim]) / total
            if part == 0:
                out_ref[here * heads_here + h, start : start + tile, :] = result.astype(jnp.bfloat16)
            else:
                out_away[h, start : start + tile, :] = result.astype(jnp.bfloat16)
        return carry

    returns = []

    def own_step(group):
        for copy in group_copies[group]:
            copy.wait_recv()
        if group + 2 < groups:
            for copy in group_copies[group + 2]:
                copy.start()
        lax.fori_loop(group * group_heads, (group + 1) * group_heads, attend_own, 0)

    def near_step(group):
        lax.fori_loop(group * group_heads, (group + 1) * group_heads, attend_near, 0)
        copy = remote(
            out_away.at[pl.ds(group * group_heads, group_heads)],
            out_ref.at[pl.ds(here * heads_here + group * group_heads, group_heads)],
            pair_send, pair_recv, 1 + 2 * groups + group, pair,
        )
        copy.start()
        returns.append(copy)

    for group in range(3):
        hop_copies[group].wait_recv()
        hop_copies[group + 1].start()
        own_step(group)
    for copy in near_first + near_second:
        copy.wait_recv()
    hop_copies[3].wait_recv()
    near_step(0)
    near_step(1)
    own_step(3)
    near_step(2)
    near_step(3)
    lead.wait_send()
    for copy in near_first + near_second + hop_copies:
        copy.wait_send()
    for copies in group_copies:
        for copy in copies:
            copy.wait_send()
    for copy in returns:
        copy.wait()


def local_pair(queries, keys, values, block_mask, strides, offsets):
    frames = lax.axis_size("frame")
    here = lax.axis_index("head")
    frame = lax.axis_index("frame")
    rows, heads, head_dim = queries.shape
    frame_blocks = block_mask.shape[1]
    part_blocks = frame_blocks // 2
    block_rows = rows // part_blocks
    heads_here = heads // 2
    groups = 4
    wide, narrow = frame_blocks // 4, frame_blocks // 2
    factor = head_dim ** (-0.5) * math.log2(math.e)

    table = [(0, half, slot, 0) for half in range(2) for slot in range(part_blocks)]
    for distance in (1, 2, 3):
        for sign in (1, -1):
            for half in range(2):
                for slot in [0, wide] if distance == 1 else [0]:
                    table.append((-sign * distance, half, slot, distance))
    table += [(gap, 0, 0, frames) for gap in range(4, frames - 3)]
    shift, half, slot, kind = (jnp.asarray(column, jnp.int32) for column in np.array(table).T)
    near_slots = len(table) - frame_blocks
    frame_ids = jnp.arange(frames, dtype=jnp.int32)

    def looked_up(array, index):
        return jnp.sum(jnp.where(index[:, None] == frame_ids[None, :], array[None, :], 0), axis=1)

    source = lax.rem(frame + shift + frames, frames)
    phase = looked_up(offsets, source)
    turn = lax.rem(narrow - lax.rem(phase, narrow), narrow)
    anchor = lax.rem(frame_blocks - lax.rem(phase, frame_blocks), frame_blocks)
    part = jnp.where(half == 0, here, 1 - here)
    ids = jnp.where(kind == frames, anchor, part * part_blocks + lax.rem(turn + slot, part_blocks))
    gap = jnp.abs(frame - source)
    spacing = jnp.where(gap == kind, looked_up(strides, gap), frame_blocks)
    flags = (kind == 0) | (lax.rem(ids + phase, spacing) == 0)
    steps = part_blocks.bit_length() - 1
    powers = jnp.asarray([2**step for step in range(steps)] + [0], jnp.int32)
    bits = jnp.where(
        powers > 0,
        lax.rem(turn[0] // jnp.maximum(powers, 1), 2),
        (anchor[0] // part_blocks == here).astype(jnp.int32),
    )

    own_mask = lax.dynamic_index_in_dim(block_mask, frame, 0, keepdims=False)
    swapped = jnp.concatenate([own_mask[part_blocks:], own_mask[:part_blocks]], axis=0)
    own_mask = jnp.where(here == 0, own_mask, swapped)
    block_ids = jnp.arange(frame_blocks, dtype=jnp.int32)
    picks = ids[:, None, None] == block_ids[None, None, :]
    kept = jnp.sum(jnp.where(picks, own_mask[None, :, :], 0), axis=2) == 1
    mask = jnp.where(kept & flags[:, None], 0.0, masked_score).astype(jnp.float32)
    mask = jnp.pad(mask, ((0, 0), (0, lanes - frame_blocks)))

    bf16 = jnp.bfloat16
    near_rows = near_slots * block_rows
    all_rows = 2 * rows
    vmem = pl.BlockSpec(memory_space=pltpu.VMEM)
    smem = pl.BlockSpec(memory_space=pltpu.SMEM)
    pair_count = 1 + 3 * groups
    dma = pltpu.SemaphoreType.DMA
    total_rows = all_rows + near_rows
    output = pl.pallas_call(
        functools.partial(fused_kernel, groups, min(256, rows), factor, near_slots),
        out_shape=jax.ShapeDtypeStruct((heads, rows, head_dim), bf16),
        in_specs=[smem, vmem, vmem, vmem, vmem],
        out_specs=vmem,
        scratch_shapes=[
            pltpu.VMEM((2, heads, 2, rows // 2, head_dim), bf16),
            pltpu.VMEM((2, heads_here, 2, rows // 2, head_dim), bf16),
            pltpu.VMEM((heads_here, rows, head_dim), bf16),
            pltpu.VMEM((2, 2, 2, heads_here, 2, block_rows, head_dim), bf16),
            pltpu.VMEM((4, 2, 2, heads_here, block_rows, head_dim), bf16),
            pltpu.VMEM((2, 2, 2, 2, 2, heads_here, block_rows, head_dim), bf16),
            pltpu.VMEM((heads_here, all_rows, 2 * head_dim), jnp.float32),
            pltpu.VMEM((heads_here, rows, head_dim), bf16),
            pltpu.VMEM((all_rows, lanes), bf16),
            pltpu.VMEM((near_rows, lanes), bf16),
            dma((pair_count,)),
            dma((pair_count,)),
            dma((12,)),
            dma((12,)),
            dma((4,)),
            dma((4,)),
        ],
        compiler_params=pltpu.CompilerParams(
            collective_id=0, has_side_effects=True, vmem_limit_bytes=56 * 1024 * 1024
        ),
        cost_estimate=pl.CostEstimate(
            flops=heads_here * 8 * all_rows * total_rows * head_dim,
            bytes_accessed=8 * heads * rows * head_dim,
            transcendentals=heads_here * all_rows * total_rows,
        ),
    )(
        bits,
        mask,
        jnp.transpose(queries, (1, 0, 2)),
        jnp.transpose(keys, (1, 0, 2)),
        jnp.transpose(values, (1, 0, 2)),
    )
    return jnp.transpose(output, (1, 0, 2))


def solution(mesh):
    paired = mesh.shape["head"] == 2 and mesh.shape["frame"] == 16
    placed = (
        P(("frame", "head"), None, None),
        P(("frame", "head"), None, None),
        P(("frame", "head"), None, None),
        P(),
        P(),
        P(),
    )
    return jax.shard_map(
        local_pair if paired else local,
        mesh=mesh,
        in_specs=placed,
        out_specs=P(("frame", "head"), None, None),
        check_vma=False,
    )
```
